256 devices in a mesh: ctx: 32 (over x, z), head: 8 (over y, core).
Axes of the slice: x: 4, y: 4, z: 8, core: 2. Of those that a mesh axis runs over, the one named last changes fastest.
Arguments:
- queries: bfloat16 [24576, 5120], P('ctx', 'head'), may hold values from -9 to 9
- keys: bfloat16 [24576, 5120], P('ctx', 'head'), may hold values from -6 to 6
- values: bfloat16 [24576, 5120], P('ctx', 'head'), may hold values from -24 to 24
- query_label: int32 [24576, 1], P('ctx'), may hold values from 0 to 31; in each aligned block of 768 rows (0 to 767, 768 to 1535, ...) at most 48 rows name the same one
- key_label: int32 [24576, 1], P('ctx'), may hold values from 0 to 383; in each aligned block of 768 rows (0 to 767, 768 to 1535, ...) at most 4 rows name the same one
- pattern: int32 [32, 16], replicated, may hold values from 0 to 383, as said below
- out_weight: bfloat16 [5120, 5120], P('head'), may hold values from -0.125 to 0.125
Outputs:
- mixed: bfloat16 [24576, 5120], P('ctx', 'head')
The draws below stay inside these ranges and needn't reach their ends.
Inputs may be any that keep to these rules, and one draw needn't show every extreme that they name: `query_label`: among the rows of one device, at most 48 name one query cluster. `key_label`: among the rows of one device, at most 4 name one key cluster; every key cluster holds some token. `pattern`: each row names 16 different key clusters.
All inputs are finite; a program needn't handle non-finite values.
Results may differ from the reference program's by a relative error of at most 0.017.
Values may be sent and summed in bfloat16 or wider, within the bound.
No kernel may reach another device: no remote copies, remote signals or barrier semaphores. Data moves between devices by JAX's collectives and lax.ppermute only.
A program may use at most 128 MiB of HBM per device.

```python
import math
import jax
import jax.numpy as jnp
import numpy as np
from jax import lax

D = 5120
HDIM = 128
HEADS_DEV = 5
HEADS = 40
TOK_DEV = 768
TOKENS = 24576
NQC = 32
NKC = 384
SLOTQ = 48
SLOTK = 4
KSEL = 16
N_HEAD = 8


def draw_queries(key, part):
    key = jax.random.fold_in(key, 3)
    base = jnp.clip(1.5 * jax.random.normal(key, (TOKENS, HEADS * HDIM), jnp.float32), -9.0, 9.0)
    return base.astype(jnp.bfloat16)


def draw_keys(key, part):
    key = jax.random.fold_in(key, 4)
    base = jnp.clip(jax.random.normal(key, (TOKENS, HEADS * HDIM), jnp.float32), -6.0, 6.0)
    return base.astype(jnp.bfloat16)


def draw_pattern(key, part):
    key = jax.random.fold_in(key, 5)
    row_keys = jax.random.split(key, NQC)
    return jax.vmap(lambda row_key: jax.random.permutation(row_key, NKC)[:KSEL])(row_keys).astype(jnp.int32)


def strengthened(entries, rng, source, target, shards_of, factor):
    def block_of(axis_at):
        return (jnp.arange(entries.shape[axis_at]) // (entries.shape[axis_at] // shards_of)).reshape((-1,) + (1,) * (entries.ndim - 1 - axis_at))

    one_side = jax.random.permutation(rng, shards_of)[block_of(target)]
    other_side = (block_of(target) + shards_of // 2) % shards_of
    return jnp.where((block_of(source) == one_side) | (block_of(source) == other_side), factor * entries, entries)


def block_scale(key, dims, cuts, low, high):
    def one(dim, blocks):
        steps = jax.random.uniform(jax.random.fold_in(jax.random.fold_in(key, 6), dim), (blocks,), jnp.float32, low / len(cuts), high / len(cuts))
        return jnp.repeat(jnp.exp(steps), dims[dim] // blocks).reshape((-1,) + (1,) * (len(dims) - dim - 1))

    loudness = one(*cuts[0])
    for cut in cuts[1:]:
        loudness = loudness * one(*cut)
    return loudness


def assign_block(rng, own, number, rows, count, top, bound, skew):
    ranking = jax.random.permutation(rng, count)
    packed, common = shares(count, rows * top, bound, skew, True), shares(count, rows * top, bound, skew, False)
    places = jnp.arange(count)

    def named(sizes, turn):
        used = int((sizes > 0).sum())
        fixed = max(1, used // 4)
        shifted = fixed + (places - fixed + turn * (used - fixed)) % max(1, count - fixed)
        return jnp.zeros((count,), jnp.int32).at[ranking[jnp.where(places < fixed, places, shifted)]].set(jnp.asarray(sizes, jnp.int32))

    sizes = jnp.where(number % 4 == 0, named(packed, number // 4), named(common, number - number // 4 - 1))
    mixed = jax.random.permutation(jax.random.fold_in(own, 3), count)
    giver, taker = mixed[0:count // 2 * 2:2], mixed[1:count // 2 * 2:2]
    margin = jnp.minimum(sizes[giver] - 1, bound - sizes[taker]) // 2
    margin = jnp.where((giver == ranking[0]) | (taker == ranking[0]) | (sizes[taker] == 0), 0, jnp.maximum(margin, 0))
    shifted = jax.random.randint(jax.random.fold_in(own, 4), (count // 2,), 0, 1 << 20) % (margin + 1)
    sizes = sizes.at[giver].add(-shifted).at[taker].add(shifted)
    members = jnp.searchsorted(jnp.cumsum(sizes), jnp.arange(rows * top), side="right").astype(jnp.int32)
    listing = members.reshape(top, rows).T
    listing = listing[jax.random.permutation(jax.random.fold_in(own, 1), rows)]
    turn = jax.random.randint(jax.random.fold_in(own, 2), (rows, 1), 0, top)
    return jnp.take_along_axis(listing, (jnp.arange(top)[None, :] + turn) % top, axis=1)


def shares(count, total, bound, skew, full):
    weights = [(1 << 20) // math.isqrt(standing ** skew) + 1 for standing in range(1, count + 1)]
    largest = bound if full else min(bound, max(-(-total // count), total * weights[0] // sum(weights)))
    least = 1 if total - largest >= count - 1 else 0
    counts, surplus = [largest] + [least] * (count - 1), total - largest - least * (count - 1)
    while surplus > 0:
        candidates = [i for i in range(1, count) if counts[i] < largest] or [i for i in range(1, count) if counts[i] < bound]
        whole, left = sum([weights[i] for i in candidates]), surplus
        for i in candidates:
            extra = min(bound - counts[i], max(1, left * weights[i] // whole), surplus)
            counts[i] = counts[i] + extra
            surplus = surplus - extra
    return np.array(counts)


def gaussian(key, dims, spread, bound, cuts=(), kind=jnp.bfloat16):
    drawn = spread * jax.random.normal(key, dims, jnp.float32)
    if cuts:
        drawn = drawn * block_scale(key, dims, cuts, -0.22, 0.18)
    return jnp.clip(drawn, -bound, bound).astype(kind)


def noise_with(stream_key, shape, deviation, limit, cuts, heavy, held_as=jnp.bfloat16):
    drawn = deviation * jax.random.normal(stream_key, shape, jnp.float32)
    if cuts:
        drawn = drawn * block_scale(stream_key, shape, cuts, -0.22, 0.18)
    return jnp.clip(strengthened(drawn, jax.random.fold_in(stream_key, 3), *heavy), -limit, limit).astype(held_as)


def setup_inputs(seed: int = 0) -> dict:
    key_list = jax.random.split(jax.random.key(seed), 8)
    queries = draw_queries(jax.random.fold_in(key_list[7], 71), 0)
    keys = draw_keys(jax.random.fold_in(key_list[7], 71), 0)
    values = gaussian(key_list[2], (TOKENS, HEADS * HDIM), 4.0, 24.0, ((0, 32), (1, 8)))
    query_label_keys = jax.random.split(jax.random.fold_in(key_list[3], 1), TOKENS // TOK_DEV)
    query_label_turns = jax.random.permutation(jax.random.fold_in(key_list[3], 3), TOKENS // TOK_DEV)
    query_label = jax.vmap(lambda own, number: assign_block(jax.random.fold_in(key_list[3], 2), own, number, TOK_DEV, NQC, 1, SLOTQ, 2))(query_label_keys, query_label_turns).reshape((TOKENS, 1))
    key_label_keys = jax.random.split(jax.random.fold_in(key_list[4], 1), TOKENS // TOK_DEV)
    key_label_turns = jax.random.permutation(jax.random.fold_in(key_list[4], 3), TOKENS // TOK_DEV)
    key_label = jax.vmap(lambda own, number: assign_block(jax.random.fold_in(key_list[4], 2), own, number, TOK_DEV, NKC, 1, SLOTK, 1))(key_label_keys, key_label_turns).reshape((TOKENS, 1))
    pattern = draw_pattern(jax.random.fold_in(key_list[7], 71), 0)
    out_weight = noise_with(key_list[6], (HEADS * HDIM, D), (HEADS * HDIM) ** -0.5, 0.125, ((0, 8),), (0, 1, 8, 2.0))
    return dict(queries=queries, keys=keys, values=values, query_label=query_label, key_label=key_label, pattern=pattern, out_weight=out_weight)


def reference(queries, keys, values, query_label, key_label, pattern, out_weight):
    query_ids = query_label[:, 0].astype(jnp.int32)
    key_ids = key_label[:, 0].astype(jnp.int32)
    query_order = jnp.argsort(query_ids, stable=True).astype(jnp.int32)
    key_order = jnp.argsort(key_ids, stable=True).astype(jnp.int32)
    query_count = lax.optimization_barrier(jnp.sum((query_ids[:, None] == jnp.arange(NQC, dtype=jnp.int32)[None, :]).astype(jnp.int32), axis=0))
    key_count = lax.optimization_barrier(jnp.sum((key_ids[:, None] == jnp.arange(NKC, dtype=jnp.int32)[None, :]).astype(jnp.int32), axis=0))
    query_start = (jnp.cumsum(query_count) - query_count).astype(jnp.int32)
    key_start = (jnp.cumsum(key_count) - key_count).astype(jnp.int32)
    query_span = 2 * TOK_DEV
    key_span = 128
    width = HEADS * HDIM
    factor = 1.0 / math.sqrt(HDIM)

    def one_cluster(cluster):
        offsets = jnp.arange(query_span, dtype=jnp.int32)
        query_live = offsets < query_count[cluster]
        query_tok = query_order[jnp.clip(query_start[cluster] + offsets, 0, TOKENS - 1).astype(jnp.int32)]
        groups = pattern[cluster].astype(jnp.int32)
        key_offsets = jnp.arange(key_span, dtype=jnp.int32)
        key_pos = jnp.clip(key_start[groups][:, None] + key_offsets[None, :], 0, TOKENS - 1).astype(jnp.int32).reshape(-1)
        key_live = (key_offsets[None, :] < key_count[groups][:, None]).reshape(-1)
        key_tok = key_order[key_pos]
        query_rows = queries[query_tok].astype(jnp.float32).reshape(query_span, HEADS, HDIM)
        key_rows = keys[key_tok].astype(jnp.float32).reshape(-1, HEADS, HDIM)
        value_rows = values[key_tok].astype(jnp.float32).reshape(-1, HEADS, HDIM)
        scores = jnp.einsum('qhd,khd->hqk', query_rows, key_rows) * factor
        scores = jnp.where(key_live[None, None, :], scores, -1e+30)
        peak = lax.optimization_barrier(jnp.max(scores, axis=2, keepdims=True))
        expon = jnp.exp(scores - peak)
        weights = (expon / lax.optimization_barrier(jnp.sum(expon, axis=2, keepdims=True))).astype(jnp.bfloat16)
        result = jnp.einsum('hqk,khd->qhd', weights.astype(jnp.float32), value_rows).astype(jnp.bfloat16)
        target = jnp.where(query_live, query_tok, TOKENS).astype(jnp.int32)
        return (target, result.reshape(query_span, width))
    targets, outputs = lax.map(one_cluster, jnp.arange(NQC, dtype=jnp.int32))
    attended = jnp.zeros((TOKENS + 1, width), jnp.bfloat16).at[targets.reshape(-1)].set(outputs.reshape(-1, width))[:TOKENS]
    group_width = HEADS_DEV * HDIM
    total = jnp.zeros((TOKENS, D), jnp.float32)
    for group in range(N_HEAD):
        lower = group * group_width
        partial_value = jnp.dot(attended[:, lower:lower + group_width], out_weight[lower:lower + group_width], preferred_element_type=jnp.float32)
        rounded = lax.optimization_barrier(partial_value.astype(jnp.bfloat16))
        total = total + rounded.astype(jnp.float32)
    return total.astype(jnp.bfloat16)
```

```python
import functools
import math

import jax
import jax.numpy as jnp
from jax import lax
from jax.experimental import pallas as pl
from jax.experimental.pallas import tpu as pltpu
from jax.sharding import PartitionSpec as P

HDIM = 128
PICKS_HERE = 4
KEEP = 40
STEP = 8
DEAD = 64.0
ALARM = 256.0
CHUNKS = ((0, 3), (3, 5))
F32, BF16 = jnp.float32, jnp.bfloat16


def params(*kinds):
    return pltpu.CompilerParams(
        dimension_semantics=kinds or None, vmem_limit_bytes=56 * 1024 * 1024
    )


def cost(flops, moved, exps=0):
    return pl.CostEstimate(flops=int(flops), bytes_accessed=int(moved), transcendentals=int(exps))


def plan_kernel(slots, qlab_ref, klab_ref, pattern_ref, qpos_ref, kpos_ref, kcount_ref, most_ref, code_ref):
    owners, rows = qpos_ref.shape
    owner = lax.broadcasted_iota(jnp.int32, (owners, rows), 0)
    q_in = qlab_ref[...] == owner
    klab = jnp.broadcast_to(klab_ref[...], (owners, rows))
    pattern = pattern_ref[...]
    k_in = klab == pattern[:, 0:1]
    for j in range(1, pattern.shape[1]):
        k_in = jnp.logical_or(k_in, klab == pattern[:, j : j + 1])
    earlier = (
        lax.broadcasted_iota(jnp.int32, (rows, rows), 0) < lax.broadcasted_iota(jnp.int32, (rows, rows), 1)
    ).astype(F32).astype(BF16)
    q_one = q_in.astype(F32)
    k_one = k_in.astype(F32)
    both = jnp.concatenate([q_one, k_one], axis=0).astype(BF16)
    before = jnp.dot(both, earlier, preferred_element_type=F32)
    q_before, k_before = before[:owners], before[owners:]
    qpos_ref[...] = jnp.where(q_in, q_before, -1.0).astype(jnp.int32)
    kpos_ref[...] = jnp.where(k_in, k_before, -1.0).astype(jnp.int32)
    counts = jnp.sum(k_one, axis=1, keepdims=True)
    kcount_ref[...] = jnp.broadcast_to(counts, kcount_ref.shape).astype(jnp.int32)
    most_ref[...] = jnp.broadcast_to(
        jnp.max(counts, axis=0, keepdims=True), most_ref.shape
    ).astype(jnp.int32)
    named = lax.broadcasted_iota(jnp.int32, (owners, 128), 0).astype(F32).astype(BF16)
    over_owner = (((0,), (0,)), ((), ()))
    label_col = lax.dot_general(q_one.astype(BF16), named, over_owner, preferred_element_type=F32)
    place_col = lax.dot_general(
        (q_one * q_before).astype(BF16),
        jnp.ones((owners, 128), BF16),
        over_owner,
        preferred_element_type=F32,
    )
    code_ref[...] = (label_col * slots + place_col).astype(jnp.int32)


def plan(qlab, klab, pattern, slots):
    owners, rows = pattern.shape[0], qlab.shape[1]
    return pl.pallas_call(
        functools.partial(plan_kernel, slots),
        out_shape=(
            jax.ShapeDtypeStruct((owners, rows), jnp.int32),
            jax.ShapeDtypeStruct((owners, rows), jnp.int32),
            jax.ShapeDtypeStruct((owners, 128), jnp.int32),
            jax.ShapeDtypeStruct((8, 128), jnp.int32),
            jax.ShapeDtypeStruct((rows, 128), jnp.int32),
        ),
        compiler_params=params(),
        cost_estimate=cost(4 * owners * rows * rows, 1 << 20),
        name="plan",
    )(qlab, klab, pattern)


def picked(pos_ref, slots):
    slot = lax.broadcasted_iota(jnp.int32, (slots, pos_ref.shape[1]), 0)
    parts = [jnp.where(pos_ref[i : i + 1, :] == slot, 1.0, 0.0) for i in range(STEP)]
    return jnp.concatenate(parts, axis=0).astype(BF16)


def pack_kernel(columns, qslots, kslots, *refs):
    qpos_ref, kpos_ref, kcount_ref, most_ref, q_ref, k_ref, v_ref, out_ref = refs
    width = out_ref.shape[2]
    if qslots:
        q_rows = jnp.dot(picked(qpos_ref, qslots), q_ref[:, columns], preferred_element_type=F32)
    pick = picked(kpos_ref, kslots)
    k_rows = jnp.dot(pick, k_ref[:, columns], preferred_element_type=F32)
    v_rows = jnp.dot(pick, v_ref[:, columns], preferred_element_type=F32)
    slot = lax.broadcasted_iota(jnp.int32, (kslots, width), 0)
    fits = most_ref[0:1, 0:1] <= kslots
    for i in range(STEP):
        live = slot < kcount_ref[i : i + 1, 0:1]
        mine = [
            jnp.where(fits, jnp.where(live, k_rows[i * kslots : (i + 1) * kslots], DEAD), ALARM),
            v_rows[i * kslots : (i + 1) * kslots],
        ]
        if qslots:
            mine.insert(0, q_rows[i * qslots : (i + 1) * qslots])
        out_ref[i] = jnp.concatenate(mine, axis=0).astype(BF16)


def pack(qpos, kpos, kcount, most, queries, keys, values, chunk, qslots, kslots):
    owners, rows = qpos.shape
    width = (chunk[1] - chunk[0]) * HDIM
    data = pl.BlockSpec((rows, queries.shape[1]), lambda i: (0, 0))
    total = qslots + 2 * kslots
    columns = slice(chunk[0] * HDIM, chunk[1] * HDIM)
    return pl.pallas_call(
        functools.partial(pack_kernel, columns, qslots, kslots),
        grid=(owners // STEP,),
        in_specs=[
            pl.BlockSpec((STEP, rows), lambda i: (i, 0)),
            pl.BlockSpec((STEP, rows), lambda i: (i, 0)),
            pl.BlockSpec((STEP, 128), lambda i: (i, 0)),
            pl.BlockSpec((8, 128), lambda i: (0, 0)),
            data,
            data,
            data,
        ],
        out_specs=pl.BlockSpec((STEP, total, width), lambda i: (i, 0, 0)),
        out_shape=jax.ShapeDtypeStruct((owners, total, width), BF16),
        compiler_params=params("arbitrary"),
        cost_estimate=cost(2 * owners * total * rows * width, 2 * owners * total * width),
        name="pack",
    )(qpos, kpos, kcount, most, queries, keys, values)


def attend_kernel(qslots, kslots, sources, over_ref, got_ref, extra_ref, out_ref, key_ref, value_ref):
    block = pl.program_id(1)
    over = over_ref[0]
    members = got_ref.shape[0]
    base = members * kslots

    def lay(rows, slots):
        rows = rows.astype(F32)
        keys = rows[:, :slots, :].reshape(-1, HDIM)
        dead = keys > DEAD / 2
        span = slice(0, members * slots)
        key_ref[span, :HDIM] = keys.astype(BF16)
        key_ref[span, HDIM:] = jnp.where(dead, -1e30, 0.0).astype(BF16)
        value_ref[span, :HDIM] = rows[:, slots:, :].reshape(-1, HDIM).astype(BF16)
        value_ref[span, HDIM:] = jnp.where(dead, 0.0, 1.0).astype(BF16)

    @pl.when(jnp.logical_and(block == 0, over == 0))
    def _():
        lay(got_ref[:, qslots:, :], kslots)

    @pl.when(jnp.logical_and(block == 0, over > 0))
    def _():
        lay(extra_ref[...], extra_ref.shape[1] // 2)

    def result(rows):
        query = got_ref[pl.ds(block * sources, sources), :qslots, :].reshape(-1, HDIM)
        query = jnp.concatenate([query, jnp.ones_like(query)], axis=1)
        scores = lax.dot_general(
            query, key_ref[:rows, :], (((1,), (1,)), ((), ())), preferred_element_type=F32
        )
        peak = jnp.max(scores, axis=1, keepdims=True)
        expon = jnp.exp2((scores - peak) * (math.log2(math.e) / math.sqrt(HDIM))).astype(BF16)
        both = jnp.dot(expon, value_ref[:rows, :], preferred_element_type=F32)
        answer = both[:, :HDIM] / both[:, HDIM:]
        out_ref[...] = answer.astype(BF16).reshape(sources, qslots, HDIM)

    @pl.when(over == 0)
    def _():
        result(base)

    @pl.when(over > 0)
    def _():
        result(key_ref.shape[0])


def attend(over, got, extra, chunk, qslots, kslots):
    members, total, width = got.shape
    heads = width // HDIM
    sources = 8
    more = extra.shape[1]
    keys = members * more // 2
    return pl.pallas_call(
        functools.partial(attend_kernel, qslots, kslots, sources),
        grid_spec=pltpu.PrefetchScalarGridSpec(
            num_scalar_prefetch=1,
            grid=(heads, members // sources),
            in_specs=[
                pl.BlockSpec((members, total, HDIM), lambda h, i, over_ref: (0, 0, h)),
                pl.BlockSpec((members, more, HDIM), lambda h, i, over_ref: (0, 0, h + chunk[0])),
            ],
            out_specs=pl.BlockSpec((sources, qslots, HDIM), lambda h, i, over_ref: (i, 0, h)),
            scratch_shapes=[
                pltpu.VMEM((keys, 2 * HDIM), BF16),
                pltpu.VMEM((keys, 2 * HDIM), BF16),
            ],
        ),
        out_shape=jax.ShapeDtypeStruct((members, qslots, width), BF16),
        compiler_params=params("arbitrary", "arbitrary"),
        cost_estimate=cost(
            8 * members * qslots * keys * width, 2 * members * total * width, members * qslots * keys * heads
        ),
        name="attend",
    )(over, got, extra)


def unpack_kernel(code_ref, got_ref, out_ref):
    rows = code_ref.shape[0]
    slots = got_ref.shape[0] * got_ref.shape[1]
    slot = lax.broadcasted_iota(jnp.int32, (rows, slots), 1)
    pick = jnp.where(code_ref[:, 0:1] == slot, 1.0, 0.0).astype(BF16)
    got = got_ref[...].reshape(slots, got_ref.shape[2])
    out_ref[...] = jnp.dot(pick, got, preferred_element_type=F32).astype(BF16)


def unpack(code, got):
    rows, width = code.shape[0], got.shape[2]
    return pl.pallas_call(
        unpack_kernel,
        out_shape=jax.ShapeDtypeStruct((rows, width), BF16),
        compiler_params=params(),
        cost_estimate=cost(2 * rows * got.shape[0] * got.shape[1] * width, 2 * got.size),
        name="unpack",
    )(code, got)


def project_kernel(rows_used, counts, *refs):
    groups, pieces = counts
    part_refs, weight_refs = refs[:pieces], refs[pieces : pieces + groups]
    out_ref, lined_ref, arrived = refs[-3:]
    first, end = rows_used
    depth = end - first

    @pl.when(pl.program_id(0) == 0)
    def _():
        copies = [
            pltpu.make_async_copy(
                weight_refs[k].at[first:end, :],
                lined_ref.at[k * depth : (k + 1) * depth, :],
                arrived.at[k],
            )
            for k in range(groups)
        ]
        for copy in copies:
            copy.start()
        for copy in copies:
            copy.wait()

    lined = jnp.concatenate([part_ref[...] for part_ref in part_refs], axis=1)
    product = jnp.dot(lined, lined_ref[...], preferred_element_type=F32)
    if len(refs) == pieces + groups + 4:
        product += refs[pieces + groups][...]
    out_ref[...] = product.astype(out_ref.dtype)


def project(parts, weights, chunk, before, kind):
    rows = parts[0].shape[0]
    groups, columns = len(weights), weights[0].shape[1]
    rows_used = (chunk[0] * HDIM, chunk[1] * HDIM)
    depth = groups * (rows_used[1] - rows_used[0])
    step = rows // 3
    block = pl.BlockSpec((step, columns), lambda i: (i, 0))
    in_specs = [pl.BlockSpec((step, part.shape[1]), lambda i: (i, 0)) for part in parts]
    in_specs += [pl.BlockSpec(memory_space=pl.ANY)] * groups
    operands = [*parts, *weights]
    if before is not None:
        in_specs.append(block)
        operands.append(before)
    return pl.pallas_call(
        functools.partial(project_kernel, rows_used, (groups, len(parts))),
        grid=(rows // step,),
        in_specs=in_specs,
        out_specs=block,
        out_shape=jax.ShapeDtypeStruct((rows, columns), kind),
        scratch_shapes=[pltpu.VMEM((depth, columns), BF16), pltpu.SemaphoreType.DMA((groups,))],
        compiler_params=params("arbitrary"),
        cost_estimate=cost(2 * rows * depth * columns, 2 * depth * (rows + columns)),
        name="project",
    )(*operands)


def shifts(groups):
    return [(along, core) for core in (0, 1) for along in range(0, groups, 2)]


def own_columns(out_weight, me, groups, which):
    columns = out_weight.shape[1] // groups
    parts = []
    for along, core in shifts(groups)[which]:
        to = lax.rem(jnp.bitwise_xor(me, core) + along, groups)
        block = lax.dynamic_slice_in_dim(out_weight, to * columns, columns, axis=1)
        if along or core:
            block = lax.ppermute(
                block, "head", [(g, ((g ^ core) + along) % groups) for g in range(groups)]
            )
        parts.append(block)
    return parts


def head_gather(rows, groups, meanwhile=None):
    def moved(part, along):
        return lax.ppermute(part, "head", [(g, (g + along) % groups) for g in range(groups)])

    cut = (rows.shape[1] // HDIM + 1) // 2 * HDIM
    after_me, before_me = moved(rows, 2), moved(rows, groups - 2)
    far = [moved(after_me[:, :cut], 2), moved(before_me[:, cut:], groups - 2)]
    if meanwhile is not None:
        after_me, before_me, meanwhile = lax.optimization_barrier((after_me, before_me, meanwhile))
    along_y = [rows, after_me, *far, before_me]
    swapped = [lax.ppermute(part, "head", [(g, g ^ 1) for g in range(groups)]) for part in along_y]
    return along_y + swapped, meanwhile


def per_device(queries, keys, values, query_label, key_label, pattern, out_weight):
    members = lax.axis_size("ctx")
    groups = lax.axis_size("head")
    me = lax.axis_index("head")
    rows = queries.shape[0]
    qslots = 2 * rows // members
    kmost = pattern.shape[1] * PICKS_HERE
    heads = queries.shape[1] // HDIM
    half = slice(0, groups // 2), slice(groups // 2, groups)
    qpos, kpos, kcount, most, code = plan(
        query_label.reshape(1, rows), key_label.reshape(1, rows), pattern, qslots
    )
    after = lax.optimization_barrier
    packed = functools.partial(pack, qpos, kpos, kcount, most, queries, keys, values)

    def exchange(block):
        return lax.all_to_all(block, "ctx", split_axis=0, concat_axis=0, tiled=True)

    def whole(over):
        return exchange(packed((0, heads), 0, kmost))

    def none(over):
        return jnp.zeros((members, 2 * kmost, heads * HDIM), BF16)

    sent0 = packed(CHUNKS[0], qslots, KEEP)
    got0 = exchange(sent0)
    sent1, late_weight = after((packed(CHUNKS[1], qslots, KEEP), out_weight))
    weights = own_columns(late_weight, me, groups, half[0])
    got0, *weights = after((got0, *weights))
    over = jnp.max((got0[:, qslots, 0:1] > (DEAD + ALARM) / 2).astype(jnp.int32), axis=0)
    extra = lax.cond(over[0] > 0, whole, none, over)
    sent1, got0, extra, late_weight = after((sent1, got0, extra, late_weight))
    got1 = exchange(sent1)
    weights += own_columns(late_weight, me, groups, half[1])
    answer0 = attend(over, got0, extra, CHUNKS[0], qslots, KEEP)
    answer0, got1, *weights = after((answer0, got1, *weights))
    back0 = exchange(answer0)
    answer1 = attend(over, got1, extra, CHUNKS[1], qslots, KEEP)
    answer1, back0 = after((answer1, back0))
    back1 = exchange(answer1)
    parts0, _ = head_gather(unpack(code, back0), groups)
    total = project(parts0, weights, CHUNKS[0], None, F32)
    parts1, total = head_gather(unpack(code, back1), groups, total)
    return project(parts1, weights, CHUNKS[1], total, BF16)


def solution(mesh):
    placed = (
        P("ctx", "head"),
        P("ctx", "head"),
        P("ctx", "head"),
        P("ctx", None),
        P("ctx", None),
        P(),
        P("head", None),
    )
    return jax.shard_map(
        per_device, mesh=mesh, in_specs=placed, out_specs=P("ctx", "head"), check_vma=False
    )
```

```python
import functools
import math

import jax
import jax.numpy as jnp
from jax import lax
from jax.experimental import pallas as pl
from jax.experimental.pallas import tpu as pltpu
from jax.sharding import PartitionSpec as P

HDIM = 128
PICKS_HERE = 4
KEEP = 40
STEP = 8
DEAD = 64.0
ALARM = 256.0
CHUNKS = ((0, 3), (3, 5))
BACK = ((0, 0, 3), (1, 3, 5))
F32, BF16 = jnp.float32, jnp.bfloat16


def params(*kinds):
    return pltpu.CompilerParams(
        dimension_semantics=kinds or None, vmem_limit_bytes=56 * 1024 * 1024
    )


def cost(flops, moved, exps=0):
    return pl.CostEstimate(flops=int(flops), bytes_accessed=int(moved), transcendentals=int(exps))


def plan_kernel(slots, qlab_ref, klab_ref, pattern_ref, qpos_ref, kpos_ref, kcount_ref, most_ref, code_ref):
    owners, rows = qpos_ref.shape
    owner = lax.broadcasted_iota(jnp.int32, (owners, rows), 0)
    q_in = qlab_ref[...] == owner
    klab = jnp.broadcast_to(klab_ref[...], (owners, rows))
    pattern = pattern_ref[...]
    k_in = klab == pattern[:, 0:1]
    for j in range(1, pattern.shape[1]):
        k_in = jnp.logical_or(k_in, klab == pattern[:, j : j + 1])
    earlier = (
        lax.broadcasted_iota(jnp.int32, (rows, rows), 0) < lax.broadcasted_iota(jnp.int32, (rows, rows), 1)
    ).astype(F32).astype(BF16)
    q_one = q_in.astype(F32)
    k_one = k_in.astype(F32)
    both = jnp.concatenate([q_one, k_one], axis=0).astype(BF16)
    before = jnp.dot(both, earlier, preferred_element_type=F32)
    q_before, k_before = before[:owners], before[owners:]
    qpos_ref[...] = jnp.where(q_in, q_before, -1.0).astype(jnp.int32)
    kpos_ref[...] = jnp.where(k_in, k_before, -1.0).astype(jnp.int32)
    counts = jnp.sum(k_one, axis=1, keepdims=True)
    kcount_ref[...] = jnp.broadcast_to(counts, kcount_ref.shape).astype(jnp.int32)
    most_ref[...] = jnp.broadcast_to(
        jnp.max(counts, axis=0, keepdims=True), most_ref.shape
    ).astype(jnp.int32)
    named = lax.broadcasted_iota(jnp.int32, (owners, 128), 0).astype(F32).astype(BF16)
    over_owner = (((0,), (0,)), ((), ()))
    label_col = lax.dot_general(q_one.astype(BF16), named, over_owner, preferred_element_type=F32)
    place_col = lax.dot_general(
        (q_one * q_before).astype(BF16),
        jnp.ones((owners, 128), BF16),
        over_owner,
        preferred_element_type=F32,
    )
    code_ref[...] = (label_col * slots + place_col).astype(jnp.int32)


def plan(qlab, klab, pattern, slots):
    owners, rows = pattern.shape[0], qlab.shape[1]
    return pl.pallas_call(
        functools.partial(plan_kernel, slots),
        out_shape=(
            jax.ShapeDtypeStruct((owners, rows), jnp.int32),
            jax.ShapeDtypeStruct((owners, rows), jnp.int32),
            jax.ShapeDtypeStruct((owners, 128), jnp.int32),
            jax.ShapeDtypeStruct((8, 128), jnp.int32),
            jax.ShapeDtypeStruct((rows, 128), jnp.int32),
        ),
        compiler_params=params(),
        cost_estimate=cost(4 * owners * rows * rows, 1 << 20),
        name="plan",
    )(qlab, klab, pattern)


def picked(pos_ref, slots):
    slot = lax.broadcasted_iota(jnp.int32, (slots, pos_ref.shape[1]), 0)
    parts = [jnp.where(pos_ref[i : i + 1, :] == slot, 1.0, 0.0) for i in range(STEP)]
    return jnp.concatenate(parts, axis=0).astype(BF16)


def pack_kernel(columns, qslots, kslots, *refs):
    qpos_ref, kpos_ref, kcount_ref, most_ref, q_ref, k_ref, v_ref, out_ref = refs
    width = out_ref.shape[2]
    if qslots:
        q_rows = jnp.dot(picked(qpos_ref, qslots), q_ref[:, columns], preferred_element_type=F32)
    pick = picked(kpos_ref, kslots)
    k_rows = jnp.dot(pick, k_ref[:, columns], preferred_element_type=F32)
    v_rows = jnp.dot(pick, v_ref[:, columns], preferred_element_type=F32)
    slot = lax.broadcasted_iota(jnp.int32, (kslots, width), 0)
    fits = most_ref[0:1, 0:1] <= kslots
    for i in range(STEP):
        live = slot < kcount_ref[i : i + 1, 0:1]
        mine = [
            jnp.where(fits, jnp.where(live, k_rows[i * kslots : (i + 1) * kslots], DEAD), ALARM),
            v_rows[i * kslots : (i + 1) * kslots],
        ]
        if qslots:
            mine.insert(0, q_rows[i * qslots : (i + 1) * qslots])
        out_ref[i] = jnp.concatenate(mine, axis=0).astype(BF16)


def pack(qpos, kpos, kcount, most, queries, keys, values, chunk, qslots, kslots):
    owners, rows = qpos.shape
    width = (chunk[1] - chunk[0]) * HDIM
    data = pl.BlockSpec((rows, queries.shape[1]), lambda i: (0, 0))
    total = qslots + 2 * kslots
    columns = slice(chunk[0] * HDIM, chunk[1] * HDIM)
    return pl.pallas_call(
        functools.partial(pack_kernel, columns, qslots, kslots),
        grid=(owners // STEP,),
        in_specs=[
            pl.BlockSpec((STEP, rows), lambda i: (i, 0)),
            pl.BlockSpec((STEP, rows), lambda i: (i, 0)),
            pl.BlockSpec((STEP, 128), lambda i: (i, 0)),
            pl.BlockSpec((8, 128), lambda i: (0, 0)),
            data,
            data,
            data,
        ],
        out_specs=pl.BlockSpec((STEP, total, width), lambda i: (i, 0, 0)),
        out_shape=jax.ShapeDtypeStruct((owners, total, width), BF16),
        compiler_params=params("arbitrary"),
        cost_estimate=cost(2 * owners * total * rows * width, 2 * owners * total * width),
        name="pack",
    )(qpos, kpos, kcount, most, queries, keys, values)


def attend_kernel(qslots, kslots, sources, over_ref, got_ref, extra_ref, out_ref, key_ref, value_ref):
    block = pl.program_id(1)
    over = over_ref[0]
    members = got_ref.shape[0]
    base = members * kslots

    def lay(rows, slots):
        rows = rows.astype(F32)
        keys = rows[:, :slots, :].reshape(-1, HDIM)
        dead = keys > DEAD / 2
        span = slice(0, members * slots)
        key_ref[span, :HDIM] = keys.astype(BF16)
        key_ref[span, HDIM:] = jnp.where(dead, -1e30, 0.0).astype(BF16)
        value_ref[span, :HDIM] = rows[:, slots:, :].reshape(-1, HDIM).astype(BF16)
        value_ref[span, HDIM:] = jnp.where(dead, 0.0, 1.0).astype(BF16)

    @pl.when(jnp.logical_and(block == 0, over == 0))
    def _():
        lay(got_ref[:, qslots:, :], kslots)

    @pl.when(jnp.logical_and(block == 0, over > 0))
    def _():
        lay(extra_ref[...], extra_ref.shape[1] // 2)

    def result(rows):
        query = got_ref[pl.ds(block * sources, sources), :qslots, :].reshape(-1, HDIM)
        query = jnp.concatenate([query, jnp.ones_like(query)], axis=1)
        scores = lax.dot_general(
            query, key_ref[:rows, :], (((1,), (1,)), ((), ())), preferred_element_type=F32
        )
        peak = jnp.max(scores, axis=1, keepdims=True)
        expon = jnp.exp2((scores - peak) * (math.log2(math.e) / math.sqrt(HDIM))).astype(BF16)
        both = jnp.dot(expon, value_ref[:rows, :], preferred_element_type=F32)
        answer = both[:, :HDIM] / both[:, HDIM:]
        out_ref[...] = answer.astype(BF16).reshape(sources, qslots, HDIM)

    @pl.when(over == 0)
    def _():
        result(base)

    @pl.when(over > 0)
    def _():
        result(key_ref.shape[0])


def attend(over, got, extra, start, chunk, qslots, kslots):
    members, total, _ = got.shape
    heads = chunk[1] - chunk[0]
    width = heads * HDIM
    sources = 8
    more = extra.shape[1]
    keys = members * more // 2
    return pl.pallas_call(
        functools.partial(attend_kernel, qslots, kslots, sources),
        grid_spec=pltpu.PrefetchScalarGridSpec(
            num_scalar_prefetch=1,
            grid=(heads, members // sources),
            in_specs=[
                pl.BlockSpec((members, total, HDIM), lambda h, i, over_ref: (0, 0, h + chunk[0] - start)),
                pl.BlockSpec((members, more, HDIM), lambda h, i, over_ref: (0, 0, h + chunk[0])),
            ],
            out_specs=pl.BlockSpec((sources, qslots, HDIM), lambda h, i, over_ref: (i, 0, h)),
            scratch_shapes=[
                pltpu.VMEM((keys, 2 * HDIM), BF16),
                pltpu.VMEM((keys, 2 * HDIM), BF16),
            ],
        ),
        out_shape=jax.ShapeDtypeStruct((members, qslots, width), BF16),
        compiler_params=params("arbitrary", "arbitrary"),
        cost_estimate=cost(
            8 * members * qslots * keys * width, 2 * members * total * width, members * qslots * keys * heads
        ),
        name="attend",
    )(over, got, extra)


def unpack_kernel(code_ref, got_ref, out_ref):
    rows = code_ref.shape[0]
    slots = got_ref.shape[0] * got_ref.shape[1]
    slot = lax.broadcasted_iota(jnp.int32, (rows, slots), 1)
    pick = jnp.where(code_ref[:, 0:1] == slot, 1.0, 0.0).astype(BF16)
    got = got_ref[...].reshape(slots, got_ref.shape[2])
    out_ref[...] = jnp.dot(pick, got, preferred_element_type=F32).astype(BF16)


def unpack(code, got):
    rows, width = code.shape[0], got.shape[2]
    return pl.pallas_call(
        unpack_kernel,
        out_shape=jax.ShapeDtypeStruct((rows, width), BF16),
        compiler_params=params(),
        cost_estimate=cost(2 * rows * got.shape[0] * got.shape[1] * width, 2 * got.size),
        name="unpack",
    )(code, got)


def project_kernel(rows_used, counts, *refs):
    groups, pieces = counts
    part_refs, weight_refs = refs[:pieces], refs[pieces : pieces + groups]
    out_ref, lined_ref, arrived = refs[-3:]
    first, end = rows_used
    depth = end - first

    @pl.when(pl.program_id(0) == 0)
    def _():
        copies = [
            pltpu.make_async_copy(
                weight_refs[k].at[first:end, :],
                lined_ref.at[k * depth : (k + 1) * depth, :],
                arrived.at[k],
            )
            for k in range(groups)
        ]
        for copy in copies:
            copy.start()
        for copy in copies:
            copy.wait()

    lined = jnp.concatenate([part_ref[...] for part_ref in part_refs], axis=1)
    product = jnp.dot(lined, lined_ref[...], preferred_element_type=F32)
    if len(refs) == pieces + groups + 4:
        product += refs[pieces + groups][...]
    out_ref[...] = product.astype(out_ref.dtype)


def project(parts, weights, chunk, before, kind):
    rows = parts[0].shape[0]
    groups, columns = len(weights), weights[0].shape[1]
    rows_used = (chunk[0] * HDIM, chunk[1] * HDIM)
    depth = groups * (rows_used[1] - rows_used[0])
    step = rows // 3
    block = pl.BlockSpec((step, columns), lambda i: (i, 0))
    in_specs = [pl.BlockSpec((step, part.shape[1]), lambda i: (i, 0)) for part in parts]
    in_specs += [pl.BlockSpec(memory_space=pl.ANY)] * groups
    operands = [*parts, *weights]
    if before is not None:
        in_specs.append(block)
        operands.append(before)
    return pl.pallas_call(
        functools.partial(project_kernel, rows_used, (groups, len(parts))),
        grid=(rows // step,),
        in_specs=in_specs,
        out_specs=block,
        out_shape=jax.ShapeDtypeStruct((rows, columns), kind),
        scratch_shapes=[pltpu.VMEM((depth, columns), BF16), pltpu.SemaphoreType.DMA((groups,))],
        compiler_params=params("arbitrary"),
        cost_estimate=cost(2 * rows * depth * columns, 2 * depth * (rows + columns)),
        name="project",
    )(*operands)


def shifts(groups):
    return [(along, core) for core in (0, 1) for along in range(0, groups, 2)]


def own_columns(out_weight, me, groups, which):
    columns = out_weight.shape[1] // groups
    parts = []
    for along, core in shifts(groups)[which]:
        to = lax.rem(jnp.bitwise_xor(me, core) + along, groups)
        block = lax.dynamic_slice_in_dim(out_weight, to * columns, columns, axis=1)
        if along or core:
            block = lax.ppermute(
                block, "head", [(g, ((g ^ core) + along) % groups) for g in range(groups)]
            )
        parts.append(block)
    return parts


def head_gather(rows, groups, meanwhile=None):
    steps = sorted(range(2, groups, 2), key=lambda along: -min(along, groups - along))
    along_y = {0: rows}
    for along in steps:
        along_y[along] = lax.ppermute(rows, "head", [(g, (g + along) % groups) for g in range(groups)])
    if meanwhile is not None:
        *held, meanwhile = lax.optimization_barrier((*[along_y[along] for along in steps], meanwhile))
        along_y.update(zip(steps, held))
    swapped = {
        along: lax.ppermute(part, "head", [(g, g ^ 1) for g in range(groups)])
        for along, part in along_y.items()
    }
    parts = [swapped[along] if core else along_y[along] for along, core in shifts(groups)]
    return parts, meanwhile


def unwritten_kernel(out_ref):
    del out_ref


def unwritten(shape):
    return pl.pallas_call(
        unwritten_kernel,
        out_specs=pl.BlockSpec(memory_space=pl.ANY),
        out_shape=jax.ShapeDtypeStruct(shape, BF16),
        compiler_params=params(),
        name="unwritten",
    )()


def per_device(queries, keys, values, query_label, key_label, pattern, out_weight):
    members = lax.axis_size("ctx")
    groups = lax.axis_size("head")
    me = lax.axis_index("head")
    rows = queries.shape[0]
    qslots = 2 * rows // members
    kmost = pattern.shape[1] * PICKS_HERE
    heads = queries.shape[1] // HDIM
    half = slice(0, groups // 2), slice(groups // 2, groups)
    qpos, kpos, kcount, most, code = plan(
        query_label.reshape(1, rows), key_label.reshape(1, rows), pattern, qslots
    )
    after = lax.optimization_barrier
    packed = functools.partial(pack, qpos, kpos, kcount, most, queries, keys, values)

    def exchange(block):
        return lax.all_to_all(block, "ctx", split_axis=0, concat_axis=0, tiled=True)

    def whole(over):
        return exchange(packed((0, heads), 0, kmost))

    def none(over):
        return unwritten((members, 2 * kmost, heads * HDIM))

    sent0 = packed(CHUNKS[0], qslots, KEEP)
    got0 = exchange(sent0)
    sent1, late_weight = after((packed(CHUNKS[1], qslots, KEEP), out_weight))
    weights = own_columns(late_weight, me, groups, half[0])
    got0, *weights = after((got0, *weights))
    over = jnp.max((got0[:, qslots, 0:1] > (DEAD + ALARM) / 2).astype(jnp.int32), axis=0)
    extra = lax.cond(over[0] > 0, whole, none, over)
    sent1, got0, extra, late_weight = after((sent1, got0, extra, late_weight))
    got1 = exchange(sent1)
    weights += own_columns(late_weight, me, groups, half[1])
    gots = got0, got1

    def attended(back):
        which, *chunk = back
        return attend(over, gots[which], extra, CHUNKS[which][0], chunk, qslots, KEEP)

    answer0 = attended(BACK[0])
    answer0, got1, *weights = after((answer0, got1, *weights))
    gots = got0, got1
    back0 = exchange(answer0)
    answer1, back0 = after((attended(BACK[1]), back0))
    back1 = exchange(answer1)
    mine1 = unpack(code, back1)
    parts0, _ = head_gather(unpack(code, back0), groups, mine1)
    total = project(parts0, weights, BACK[0][1:], None, F32)
    parts1, total = head_gather(mine1, groups, total)
    return project(parts1, weights, BACK[1][1:], total, BF16)


def solution(mesh):
    placed = (
        P("ctx", "head"),
        P("ctx", "head"),
        P("ctx", "head"),
        P("ctx", None),
        P("ctx", None),
        P(),
        P("head", None),
    )
    return jax.shard_map(
        per_device, mesh=mesh, in_specs=placed, out_specs=P("ctx", "head"), check_vma=False
    )
```

```python
import functools
import math

import jax
import jax.numpy as jnp
from jax import lax
from jax.experimental import pallas as pl
from jax.experimental.pallas import tpu as pltpu
from jax.sharding import PartitionSpec as P

HDIM = 128
PICKS_HERE = 4
KEEP = 40
STEP = 8
DEAD = 64.0
ALARM = 256.0
CHUNKS = ((0, 3), (3, 5))
BACK = ((0, 0, 3), (1, 3, 5))
F32, BF16 = jnp.float32, jnp.bfloat16


def params(*kinds):
    return pltpu.CompilerParams(
        dimension_semantics=kinds or None, vmem_limit_bytes=56 * 1024 * 1024
    )


def cost(flops, moved, exps=0):
    return pl.CostEstimate(flops=int(flops), bytes_accessed=int(moved), transcendentals=int(exps))


def plan_kernel(slots, qlab_ref, klab_ref, pattern_ref, qpos_ref, kpos_ref, kcount_ref, most_ref, code_ref):
    owners, rows = qpos_ref.shape
    owner = lax.broadcasted_iota(jnp.int32, (owners, rows), 0)
    q_in = qlab_ref[...] == owner
    klab = jnp.broadcast_to(klab_ref[...], (owners, rows))
    pattern = pattern_ref[...]
    k_in = klab == pattern[:, 0:1]
    for j in range(1, pattern.shape[1]):
        k_in = jnp.logical_or(k_in, klab == pattern[:, j : j + 1])
    earlier = (
        lax.broadcasted_iota(jnp.int32, (rows, rows), 0) < lax.broadcasted_iota(jnp.int32, (rows, rows), 1)
    ).astype(F32).astype(BF16)
    q_one = q_in.astype(F32)
    k_one = k_in.astype(F32)
    both = jnp.concatenate([q_one, k_one], axis=0).astype(BF16)
    before = jnp.dot(both, earlier, preferred_element_type=F32)
    q_before, k_before = before[:owners], before[owners:]
    qpos_ref[...] = jnp.where(q_in, q_before, -1.0).astype(jnp.int32)
    kpos_ref[...] = jnp.where(k_in, k_before, -1.0).astype(jnp.int32)
    counts = jnp.sum(k_one, axis=1, keepdims=True)
    kcount_ref[...] = jnp.broadcast_to(counts, kcount_ref.shape).astype(jnp.int32)
    most_ref[...] = jnp.broadcast_to(
        jnp.max(counts, axis=0, keepdims=True), most_ref.shape
    ).astype(jnp.int32)
    named = lax.broadcasted_iota(jnp.int32, (owners, 128), 0).astype(F32).astype(BF16)
    over_owner = (((0,), (0,)), ((), ()))
    label_col = lax.dot_general(q_one.astype(BF16), named, over_owner, preferred_element_type=F32)
    place_col = lax.dot_general(
        (q_one * q_before).astype(BF16),
        jnp.ones((owners, 128), BF16),
        over_owner,
        preferred_element_type=F32,
    )
    code_ref[...] = (label_col * slots + place_col).astype(jnp.int32)


def plan(qlab, klab, pattern, slots):
    owners, rows = pattern.shape[0], qlab.shape[1]
    return pl.pallas_call(
        functools.partial(plan_kernel, slots),
        out_shape=(
            jax.ShapeDtypeStruct((owners, rows), jnp.int32),
            jax.ShapeDtypeStruct((owners, rows), jnp.int32),
            jax.ShapeDtypeStruct((owners, 128), jnp.int32),
            jax.ShapeDtypeStruct((8, 128), jnp.int32),
            jax.ShapeDtypeStruct((rows, 128), jnp.int32),
        ),
        compiler_params=params(),
        cost_estimate=cost(4 * owners * rows * rows, 1 << 20),
        name="plan",
    )(qlab, klab, pattern)


def picked(pos_ref, slots):
    slot = lax.broadcasted_iota(jnp.int32, (slots, pos_ref.shape[1]), 0)
    parts = [jnp.where(pos_ref[i : i + 1, :] == slot, 1.0, 0.0) for i in range(STEP)]
    return jnp.concatenate(parts, axis=0).astype(BF16)


def pack_kernel(columns, qslots, kslots, *refs):
    qpos_ref, kpos_ref, kcount_ref, most_ref, q_ref, k_ref, v_ref, out_ref = refs
    width = out_ref.shape[2]
    if qslots:
        q_rows = jnp.dot(picked(qpos_ref, qslots), q_ref[:, columns], preferred_element_type=F32)
    pick = picked(kpos_ref, kslots)
    k_rows = jnp.dot(pick, k_ref[:, columns], preferred_element_type=F32)
    v_rows = jnp.dot(pick, v_ref[:, columns], preferred_element_type=F32)
    slot = lax.broadcasted_iota(jnp.int32, (kslots, width), 0)
    fits = most_ref[0:1, 0:1] <= kslots
    for i in range(STEP):
        live = slot < kcount_ref[i : i + 1, 0:1]
        mine = [
            jnp.where(fits, jnp.where(live, k_rows[i * kslots : (i + 1) * kslots], DEAD), ALARM),
            v_rows[i * kslots : (i + 1) * kslots],
        ]
        if qslots:
            mine.insert(0, q_rows[i * qslots : (i + 1) * qslots])
        out_ref[i] = jnp.concatenate(mine, axis=0).astype(BF16)


def pack(qpos, kpos, kcount, most, queries, keys, values, chunk, qslots, kslots):
    owners, rows = qpos.shape
    width = (chunk[1] - chunk[0]) * HDIM
    data = pl.BlockSpec((rows, queries.shape[1]), lambda i: (0, 0))
    total = qslots + 2 * kslots
    columns = slice(chunk[0] * HDIM, chunk[1] * HDIM)
    return pl.pallas_call(
        functools.partial(pack_kernel, columns, qslots, kslots),
        grid=(owners // STEP,),
        in_specs=[
            pl.BlockSpec((STEP, rows), lambda i: (i, 0)),
            pl.BlockSpec((STEP, rows), lambda i: (i, 0)),
            pl.BlockSpec((STEP, 128), lambda i: (i, 0)),
            pl.BlockSpec((8, 128), lambda i: (0, 0)),
            data,
            data,
            data,
        ],
        out_specs=pl.BlockSpec((STEP, total, width), lambda i: (i, 0, 0)),
        out_shape=jax.ShapeDtypeStruct((owners, total, width), BF16),
        compiler_params=params("arbitrary"),
        cost_estimate=cost(2 * owners * total * rows * width, 2 * owners * total * width),
        name="pack",
    )(qpos, kpos, kcount, most, queries, keys, values)


def attend_kernel(qslots, kslots, sources, over_ref, got_ref, extra_ref, out_ref, key_ref, value_ref):
    block = pl.program_id(1)
    over = over_ref[0]
    members = got_ref.shape[0]
    base = members * kslots

    def lay(rows, slots):
        rows = rows.astype(F32)
        keys = rows[:, :slots, :].reshape(-1, HDIM)
        dead = keys > DEAD / 2
        span = slice(0, members * slots)
        key_ref[span, :HDIM] = keys.astype(BF16)
        key_ref[span, HDIM:] = jnp.where(dead, -1e30, 0.0).astype(BF16)
        value_ref[span, :HDIM] = rows[:, slots:, :].reshape(-1, HDIM).astype(BF16)
        value_ref[span, HDIM:] = jnp.where(dead, 0.0, 1.0).astype(BF16)

    @pl.when(jnp.logical_and(block == 0, over == 0))
    def _():
        lay(got_ref[:, qslots:, :], kslots)

    @pl.when(jnp.logical_and(block == 0, over > 0))
    def _():
        lay(extra_ref[...], extra_ref.shape[1] // 2)

    def result(rows):
        query = got_ref[pl.ds(block * sources, sources), :qslots, :].reshape(-1, HDIM)
        query = jnp.concatenate([query, jnp.ones_like(query)], axis=1)
        scores = lax.dot_general(
            query, key_ref[:rows, :], (((1,), (1,)), ((), ())), preferred_element_type=F32
        )
        peak = jnp.max(scores, axis=1, keepdims=True)
        expon = jnp.exp2((scores - peak) * (math.log2(math.e) / math.sqrt(HDIM))).astype(BF16)
        both = jnp.dot(expon, value_ref[:rows, :], preferred_element_type=F32)
        answer = both[:, :HDIM] / both[:, HDIM:]
        out_ref[...] = answer.astype(BF16).reshape(sources, qslots, HDIM)

    @pl.when(over == 0)
    def _():
        result(base)

    @pl.when(over > 0)
    def _():
        result(key_ref.shape[0])


def attend(over, got, extra, start, chunk, qslots, kslots):
    members, total, _ = got.shape
    heads = chunk[1] - chunk[0]
    width = heads * HDIM
    sources = 8
    more = extra.shape[1]
    keys = members * more // 2
    return pl.pallas_call(
        functools.partial(attend_kernel, qslots, kslots, sources),
        grid_spec=pltpu.PrefetchScalarGridSpec(
            num_scalar_prefetch=1,
            grid=(heads, members // sources),
            in_specs=[
                pl.BlockSpec((members, total, HDIM), lambda h, i, over_ref: (0, 0, h + chunk[0] - start)),
                pl.BlockSpec((members, more, HDIM), lambda h, i, over_ref: (0, 0, h + chunk[0])),
            ],
            out_specs=pl.BlockSpec((sources, qslots, HDIM), lambda h, i, over_ref: (i, 0, h)),
            scratch_shapes=[
                pltpu.VMEM((keys, 2 * HDIM), BF16),
                pltpu.VMEM((keys, 2 * HDIM), BF16),
            ],
        ),
        out_shape=jax.ShapeDtypeStruct((members, qslots, width), BF16),
        compiler_params=params("arbitrary", "arbitrary"),
        cost_estimate=cost(
            8 * members * qslots * keys * width, 2 * members * total * width, members * qslots * keys * heads
        ),
        name="attend",
    )(over, got, extra)


def unpack_kernel(code_ref, got_ref, out_ref):
    rows = code_ref.shape[0]
    slots = got_ref.shape[0] * got_ref.shape[1]
    slot = lax.broadcasted_iota(jnp.int32, (rows, slots), 1)
    pick = jnp.where(code_ref[:, 0:1] == slot, 1.0, 0.0).astype(BF16)
    got = got_ref[...].reshape(slots, got_ref.shape[2])
    out_ref[...] = jnp.dot(pick, got, preferred_element_type=F32).astype(BF16)


def unpack(code, got):
    rows, width = code.shape[0], got.shape[2]
    return pl.pallas_call(
        unpack_kernel,
        out_shape=jax.ShapeDtypeStruct((rows, width), BF16),
        compiler_params=params(),
        cost_estimate=cost(2 * rows * got.shape[0] * got.shape[1] * width, 2 * got.size),
        name="unpack",
    )(code, got)


def project_kernel(spans, *refs):
    count = len(spans)
    part_refs, weight_refs = refs[:count], refs[count : 2 * count]
    out_ref, lined_ref, arrived = refs[-3:]

    @pl.when(pl.program_id(0) == 0)
    def _():
        copies, at = [], 0
        for k, (first, end) in enumerate(spans):
            copies.append(
                pltpu.make_async_copy(
                    weight_refs[k].at[first:end, :],
                    lined_ref.at[at : at + end - first, :],
                    arrived.at[k],
                )
            )
            at += end - first
        for copy in copies:
            copy.start()
        for copy in copies:
            copy.wait()

    lined = jnp.concatenate([part_ref[...] for part_ref in part_refs], axis=1)
    product = jnp.dot(lined, lined_ref[...], preferred_element_type=F32)
    if len(refs) == 2 * count + 4:
        product += refs[2 * count][...]
    out_ref[...] = product.astype(out_ref.dtype)


def project(items, before, kind):
    rows, columns = items[0][0].shape[0], items[0][1].shape[1]
    spans = tuple((first * HDIM, end * HDIM) for _, _, (first, end) in items)
    depth = sum(end - first for first, end in spans)
    step = rows // 2
    block = pl.BlockSpec((step, columns), lambda i: (i, 0))
    in_specs = [pl.BlockSpec((step, part.shape[1]), lambda i: (i, 0)) for part, _, _ in items]
    in_specs += [pl.BlockSpec(memory_space=pl.ANY)] * len(items)
    operands = [part for part, _, _ in items] + [weight for _, weight, _ in items]
    if before is not None:
        in_specs.append(block)
        operands.append(before)
    return pl.pallas_call(
        functools.partial(project_kernel, spans),
        grid=(rows // step,),
        in_specs=in_specs,
        out_specs=block,
        out_shape=jax.ShapeDtypeStruct((rows, columns), kind),
        scratch_shapes=[pltpu.VMEM((depth, columns), BF16), pltpu.SemaphoreType.DMA((len(items),))],
        compiler_params=params("arbitrary"),
        cost_estimate=cost(2 * rows * depth * columns, 2 * depth * (rows + columns)),
        name="project",
    )(*operands)


def shifts(groups):
    return [(along, core) for core in (0, 1) for along in range(0, groups, 2)]


def own_columns(out_weight, me, groups, which):
    columns = out_weight.shape[1] // groups
    parts = []
    for along, core in shifts(groups)[which]:
        to = lax.rem(jnp.bitwise_xor(me, core) + along, groups)
        block = lax.dynamic_slice_in_dim(out_weight, to * columns, columns, axis=1)
        if along or core:
            block = lax.ppermute(
                block, "head", [(g, ((g ^ core) + along) % groups) for g in range(groups)]
            )
        parts.append(block)
    return parts


def along_y(rows, groups):
    steps = sorted(range(2, groups, 2), key=lambda along: -min(along, groups - along))
    moved = {
        along: lax.ppermute(rows, "head", [(g, (g + along) % groups) for g in range(groups)])
        for along in steps
    }
    return [moved[along] for along in sorted(moved)]


def swapped(rows, groups):
    return lax.ppermute(rows, "head", [(g, g ^ 1) for g in range(groups)])


def unwritten_kernel(out_ref):
    del out_ref


def unwritten(shape):
    return pl.pallas_call(
        unwritten_kernel,
        out_specs=pl.BlockSpec(memory_space=pl.ANY),
        out_shape=jax.ShapeDtypeStruct(shape, BF16),
        compiler_params=params(),
        name="unwritten",
    )()


def per_device(queries, keys, values, query_label, key_label, pattern, out_weight):
    members = lax.axis_size("ctx")
    groups = lax.axis_size("head")
    me = lax.axis_index("head")
    rows = queries.shape[0]
    qslots = 2 * rows // members
    kmost = pattern.shape[1] * PICKS_HERE
    heads = queries.shape[1] // HDIM
    half = slice(0, groups // 2), slice(groups // 2, groups)
    qpos, kpos, kcount, most, code = plan(
        query_label.reshape(1, rows), key_label.reshape(1, rows), pattern, qslots
    )
    after = lax.optimization_barrier
    packed = functools.partial(pack, qpos, kpos, kcount, most, queries, keys, values)

    def exchange(block):
        return lax.all_to_all(block, "ctx", split_axis=0, concat_axis=0, tiled=True)

    def whole(over):
        return exchange(packed((0, heads), 0, kmost))

    def none(over):
        return unwritten((members, 2 * kmost, heads * HDIM))

    sent0 = packed(CHUNKS[0], qslots, KEEP)
    got0 = exchange(sent0)
    sent1, late_weight = after((packed(CHUNKS[1], qslots, KEEP), out_weight))
    weights = own_columns(late_weight, me, groups, half[0])
    got0, *weights = after((got0, *weights))
    over = jnp.max((got0[:, qslots, 0:1] > (DEAD + ALARM) / 2).astype(jnp.int32), axis=0)
    extra = lax.cond(over[0] > 0, whole, none, over)
    sent1, got0, extra, late_weight = after((sent1, got0, extra, late_weight))
    got1 = exchange(sent1)
    weights += own_columns(late_weight, me, groups, half[1])
    gots = got0, got1

    def attended(back):
        which, *chunk = back
        return attend(over, gots[which], extra, CHUNKS[which][0], chunk, qslots, KEEP)

    answer0 = attended(BACK[0])
    answer0, got1, *weights = after((answer0, got1, *weights))
    gots = got0, got1
    back0 = exchange(answer0)
    answer1, back0 = after((attended(BACK[1]), back0))
    back1 = exchange(answer1)
    mine1 = unpack(code, back1)
    mine0 = unpack(code, back0)
    own_w, y_w, other_w, far_w = weights[0], weights[1:4], weights[4], weights[5:]
    chunk0, chunk1 = BACK[0][1:], BACK[1][1:]

    def items(parts, weights, chunk):
        return [(part, weight, chunk) for part, weight in zip(parts, weights)]

    y0 = along_y(mine0, groups)
    *y0, _ = after((*y0, mine1))
    parts0 = [mine0, *y0, swapped(mine0, groups), *[swapped(part, groups) for part in y0]]
    y1 = along_y(mine1, groups)
    near1 = [mine1, swapped(mine1, groups)]
    total = project(
        items(parts0, weights, chunk0) + items(near1, [own_w, other_w], chunk1), None, F32
    )
    *y1, total = after((*y1, total))
    far1 = [swapped(part, groups) for part in y1]
    total = project(items(y1, y_w, chunk1), total, F32)
    return project(items(far1, far_w, chunk1), total, BF16)


def solution(mesh):
    placed = (
        P("ctx", "head"),
        P("ctx", "head"),
        P("ctx", "head"),
        P("ctx", None),
        P("ctx", None),
        P(),
        P("head", None),
    )
    return jax.shard_map(
        per_device, mesh=mesh, in_specs=placed, out_specs=P("ctx", "head"), check_vma=False
    )
```

```python
import functools
import math

import jax
import jax.numpy as jnp
from jax import lax
from jax.experimental import pallas as pl
from jax.experimental.pallas import tpu as pltpu
from jax.sharding import PartitionSpec as P

HDIM = 128
PICKS_HERE = 4
KEEP = 40
STEP = 8
DEAD = 64.0
ALARM = 256.0
CHUNKS = ((0, 3), (3, 5))
BACK = ((0, 0, 3), (1, 3, 5))
F32, BF16 = jnp.float32, jnp.bfloat16


def params(*kinds):
    return pltpu.CompilerParams(
        dimension_semantics=kinds or None, vmem_limit_bytes=56 * 1024 * 1024
    )


def cost(flops, moved, exps=0):
    return pl.CostEstimate(flops=int(flops), bytes_accessed=int(moved), transcendentals=int(exps))


def plan_kernel(slots, qlab_ref, klab_ref, pattern_ref, qpos_ref, kpos_ref, kcount_ref, most_ref, code_ref):
    owners, rows = qpos_ref.shape
    owner = lax.broadcasted_iota(jnp.int32, (owners, rows), 0)
    q_in = qlab_ref[...] == owner
    klab = jnp.broadcast_to(klab_ref[...], (owners, rows))
    pattern = pattern_ref[...]
    k_in = klab == pattern[:, 0:1]
    for j in range(1, pattern.shape[1]):
        k_in = jnp.logical_or(k_in, klab == pattern[:, j : j + 1])
    earlier = (
        lax.broadcasted_iota(jnp.int32, (rows, rows), 0) < lax.broadcasted_iota(jnp.int32, (rows, rows), 1)
    ).astype(F32).astype(BF16)
    q_one = q_in.astype(F32)
    k_one = k_in.astype(F32)
    both = jnp.concatenate([q_one, k_one], axis=0).astype(BF16)
    before = jnp.dot(both, earlier, preferred_element_type=F32)
    q_before, k_before = before[:owners], before[owners:]
    qpos_ref[...] = jnp.where(q_in, q_before, -1.0).astype(jnp.int32)
    kpos_ref[...] = jnp.where(k_in, k_before, -1.0).astype(jnp.int32)
    counts = jnp.sum(k_one, axis=1, keepdims=True)
    kcount_ref[...] = jnp.broadcast_to(counts, kcount_ref.shape).astype(jnp.int32)
    most_ref[...] = jnp.broadcast_to(
        jnp.max(counts, axis=0, keepdims=True), most_ref.shape
    ).astype(jnp.int32)
    named = lax.broadcasted_iota(jnp.int32, (owners, 128), 0).astype(F32).astype(BF16)
    over_owner = (((0,), (0,)), ((), ()))
    label_col = lax.dot_general(q_one.astype(BF16), named, over_owner, preferred_element_type=F32)
    place_col = lax.dot_general(
        (q_one * q_before).astype(BF16),
        jnp.ones((owners, 128), BF16),
        over_owner,
        preferred_element_type=F32,
    )
    code_ref[...] = (label_col * slots + place_col).astype(jnp.int32)


def plan(qlab, klab, pattern, slots):
    owners, rows = pattern.shape[0], qlab.shape[1]
    return pl.pallas_call(
        functools.partial(plan_kernel, slots),
        out_shape=(
            jax.ShapeDtypeStruct((owners, rows), jnp.int32),
            jax.ShapeDtypeStruct((owners, rows), jnp.int32),
            jax.ShapeDtypeStruct((owners, 128), jnp.int32),
            jax.ShapeDtypeStruct((8, 128), jnp.int32),
            jax.ShapeDtypeStruct((rows, 128), jnp.int32),
        ),
        compiler_params=params(),
        cost_estimate=cost(4 * owners * rows * rows, 1 << 20),
        name="plan",
    )(qlab, klab, pattern)


def picked(pos_ref, slots):
    slot = lax.broadcasted_iota(jnp.int32, (slots, pos_ref.shape[1]), 0)
    parts = [jnp.where(pos_ref[i : i + 1, :] == slot, 1.0, 0.0) for i in range(STEP)]
    return jnp.concatenate(parts, axis=0).astype(BF16)


def pack_kernel(columns, qslots, kslots, *refs):
    qpos_ref, kpos_ref, kcount_ref, most_ref, q_ref, k_ref, v_ref, out_ref = refs
    width = out_ref.shape[2]
    if qslots:
        q_rows = jnp.dot(picked(qpos_ref, qslots), q_ref[:, columns], preferred_element_type=F32)
    pick = picked(kpos_ref, kslots)
    k_rows = jnp.dot(pick, k_ref[:, columns], preferred_element_type=F32)
    v_rows = jnp.dot(pick, v_ref[:, columns], preferred_element_type=F32)
    slot = lax.broadcasted_iota(jnp.int32, (kslots, width), 0)
    fits = most_ref[0:1, 0:1] <= kslots
    for i in range(STEP):
        live = slot < kcount_ref[i : i + 1, 0:1]
        mine = [
            jnp.where(fits, jnp.where(live, k_rows[i * kslots : (i + 1) * kslots], DEAD), ALARM),
            v_rows[i * kslots : (i + 1) * kslots],
        ]
        if qslots:
            mine.insert(0, q_rows[i * qslots : (i + 1) * qslots])
        out_ref[i] = jnp.concatenate(mine, axis=0).astype(BF16)


def pack(qpos, kpos, kcount, most, queries, keys, values, chunk, qslots, kslots):
    owners, rows = qpos.shape
    width = (chunk[1] - chunk[0]) * HDIM
    data = pl.BlockSpec((rows, queries.shape[1]), lambda i: (0, 0))
    total = qslots + 2 * kslots
    columns = slice(chunk[0] * HDIM, chunk[1] * HDIM)
    return pl.pallas_call(
        functools.partial(pack_kernel, columns, qslots, kslots),
        grid=(owners // STEP,),
        in_specs=[
            pl.BlockSpec((STEP, rows), lambda i: (i, 0)),
            pl.BlockSpec((STEP, rows), lambda i: (i, 0)),
            pl.BlockSpec((STEP, 128), lambda i: (i, 0)),
            pl.BlockSpec((8, 128), lambda i: (0, 0)),
            data,
            data,
            data,
        ],
        out_specs=pl.BlockSpec((STEP, total, width), lambda i: (i, 0, 0)),
        out_shape=jax.ShapeDtypeStruct((owners, total, width), BF16),
        compiler_params=params("arbitrary"),
        cost_estimate=cost(2 * owners * total * rows * width, 2 * owners * total * width),
        name="pack",
    )(qpos, kpos, kcount, most, queries, keys, values)


def attend_kernel(qslots, kslots, sources, over_ref, got_ref, extra_ref, out_ref, key_ref, value_ref):
    block = pl.program_id(1)
    over = over_ref[0]
    members = got_ref.shape[0]
    base = members * kslots

    def lay(rows, slots):
        rows = rows.astype(F32)
        keys = rows[:, :slots, :].reshape(-1, HDIM)
        dead = keys > DEAD / 2
        span = slice(0, members * slots)
        key_ref[span, :HDIM] = keys.astype(BF16)
        key_ref[span, HDIM:] = jnp.where(dead, -1e30, 0.0).astype(BF16)
        value_ref[span, :HDIM] = rows[:, slots:, :].reshape(-1, HDIM).astype(BF16)
        value_ref[span, HDIM:] = jnp.where(dead, 0.0, 1.0).astype(BF16)

    @pl.when(jnp.logical_and(block == 0, over == 0))
    def _():
        lay(got_ref[:, qslots:, :], kslots)

    @pl.when(jnp.logical_and(block == 0, over > 0))
    def _():
        lay(extra_ref[...], extra_ref.shape[1] // 2)

    def result(rows):
        query = got_ref[pl.ds(block * sources, sources), :qslots, :].reshape(-1, HDIM)
        query = jnp.concatenate([query, jnp.ones_like(query)], axis=1)
        scores = lax.dot_general(
            query, key_ref[:rows, :], (((1,), (1,)), ((), ())), preferred_element_type=F32
        )
        peak = jnp.max(scores, axis=1, keepdims=True)
        expon = jnp.exp2((scores - peak) * (math.log2(math.e) / math.sqrt(HDIM))).astype(BF16)
        both = jnp.dot(expon, value_ref[:rows, :], preferred_element_type=F32)
        answer = both[:, :HDIM] / both[:, HDIM:]
        out_ref[...] = answer.astype(BF16).reshape(sources, qslots, HDIM)

    @pl.when(over == 0)
    def _():
        result(base)

    @pl.when(over > 0)
    def _():
        result(key_ref.shape[0])


def attend(over, got, extra, start, chunk, qslots, kslots):
    members, total, _ = got.shape
    heads = chunk[1] - chunk[0]
    width = heads * HDIM
    sources = 8
    more = extra.shape[1]
    keys = members * more // 2
    return pl.pallas_call(
        functools.partial(attend_kernel, qslots, kslots, sources),
        grid_spec=pltpu.PrefetchScalarGridSpec(
            num_scalar_prefetch=1,
            grid=(heads, members // sources),
            in_specs=[
                pl.BlockSpec((members, total, HDIM), lambda h, i, over_ref: (0, 0, h + chunk[0] - start)),
                pl.BlockSpec((members, more, HDIM), lambda h, i, over_ref: (0, 0, h + chunk[0])),
            ],
            out_specs=pl.BlockSpec((sources, qslots, HDIM), lambda h, i, over_ref: (i, 0, h)),
            scratch_shapes=[
                pltpu.VMEM((keys, 2 * HDIM), BF16),
                pltpu.VMEM((keys, 2 * HDIM), BF16),
            ],
        ),
        out_shape=jax.ShapeDtypeStruct((members, qslots, width), BF16),
        compiler_params=params("arbitrary", "arbitrary"),
        cost_estimate=cost(
            8 * members * qslots * keys * width, 2 * members * total * width, members * qslots * keys * heads
        ),
        name="attend",
    )(over, got, extra)


def unpack_kernel(code_ref, got_ref, out_ref):
    rows = code_ref.shape[0]
    slots = got_ref.shape[0] * got_ref.shape[1]
    slot = lax.broadcasted_iota(jnp.int32, (rows, slots), 1)
    pick = jnp.where(code_ref[:, 0:1] == slot, 1.0, 0.0).astype(BF16)
    got = got_ref[...].reshape(slots, got_ref.shape[2])
    out_ref[...] = jnp.dot(pick, got, preferred_element_type=F32).astype(BF16)


def unpack(code, got):
    rows, width = code.shape[0], got.shape[2]
    return pl.pallas_call(
        unpack_kernel,
        out_shape=jax.ShapeDtypeStruct((rows, width), BF16),
        compiler_params=params(),
        cost_estimate=cost(2 * rows * got.shape[0] * got.shape[1] * width, 2 * got.size),
        name="unpack",
    )(code, got)


def project_kernel(spans, *refs):
    count = len(spans)
    part_refs, weight_refs = refs[:count], refs[count : 2 * count]
    out_ref, lined_ref, arrived = refs[-3:]

    @pl.when(pl.program_id(0) == 0)
    def _():
        copies, at = [], 0
        for k, (first, end) in enumerate(spans):
            copies.append(
                pltpu.make_async_copy(
                    weight_refs[k].at[first:end, :],
                    lined_ref.at[at : at + end - first, :],
                    arrived.at[k],
                )
            )
            at += end - first
        for copy in copies:
            copy.start()
        for copy in copies:
            copy.wait()

    lined = jnp.concatenate([part_ref[...] for part_ref in part_refs], axis=1)
    product = jnp.dot(lined, lined_ref[...], preferred_element_type=F32)
    if len(refs) == 2 * count + 4:
        product += refs[2 * count][...]
    out_ref[...] = product.astype(out_ref.dtype)


def project(items, before, kind):
    rows, columns = items[0][0].shape[0], items[0][1].shape[1]
    spans = tuple((first * HDIM, end * HDIM) for _, _, (first, end) in items)
    depth = sum(end - first for first, end in spans)
    step = rows // 2
    block = pl.BlockSpec((step, columns), lambda i: (i, 0))
    in_specs = [pl.BlockSpec((step, part.shape[1]), lambda i: (i, 0)) for part, _, _ in items]
    in_specs += [pl.BlockSpec(memory_space=pl.ANY)] * len(items)
    operands = [part for part, _, _ in items] + [weight for _, weight, _ in items]
    if before is not None:
        in_specs.append(block)
        operands.append(before)
    return pl.pallas_call(
        functools.partial(project_kernel, spans),
        grid=(rows // step,),
        in_specs=in_specs,
        out_specs=block,
        out_shape=jax.ShapeDtypeStruct((rows, columns), kind),
        scratch_shapes=[pltpu.VMEM((depth, columns), BF16), pltpu.SemaphoreType.DMA((len(items),))],
        compiler_params=params("arbitrary"),
        cost_estimate=cost(2 * rows * depth * columns, 2 * depth * (rows + columns)),
        name="project",
    )(*operands)


def shifts(groups):
    return [(along, core) for core in (0, 1) for along in range(0, groups, 2)]


def own_columns(out_weight, me, groups, which):
    columns = out_weight.shape[1] // groups
    parts = []
    for along, core in shifts(groups)[which]:
        to = lax.rem(jnp.bitwise_xor(me, core) + along, groups)
        block = lax.dynamic_slice_in_dim(out_weight, to * columns, columns, axis=1)
        if along or core:
            block = lax.ppermute(
                block, "head", [(g, ((g ^ core) + along) % groups) for g in range(groups)]
            )
        parts.append(block)
    return parts


def along_y(rows, groups):
    steps = sorted(range(2, groups, 2), key=lambda along: -min(along, groups - along))
    moved = {
        along: lax.ppermute(rows, "head", [(g, (g + along) % groups) for g in range(groups)])
        for along in steps
    }
    return [moved[along] for along in sorted(moved)]


def swapped(rows, groups):
    return lax.ppermute(rows, "head", [(g, g ^ 1) for g in range(groups)])


def unwritten_kernel(out_ref):
    del out_ref


def unwritten(shape):
    return pl.pallas_call(
        unwritten_kernel,
        out_specs=pl.BlockSpec(memory_space=pl.ANY),
        out_shape=jax.ShapeDtypeStruct(shape, BF16),
        compiler_params=params(),
        name="unwritten",
    )()


def per_device(queries, keys, values, query_label, key_label, pattern, out_weight):
    members = lax.axis_size("ctx")
    groups = lax.axis_size("head")
    me = lax.axis_index("head")
    rows = queries.shape[0]
    qslots = 2 * rows // members
    kmost = pattern.shape[1] * PICKS_HERE
    heads = queries.shape[1] // HDIM
    half = slice(0, groups // 2), slice(groups // 2, groups)
    qpos, kpos, kcount, most, code = plan(
        query_label.reshape(1, rows), key_label.reshape(1, rows), pattern, qslots
    )
    after = lax.optimization_barrier
    packed = functools.partial(pack, qpos, kpos, kcount, most, queries, keys, values)

    def exchange(block):
        return lax.all_to_all(block, "ctx", split_axis=0, concat_axis=0, tiled=True)

    def whole(over):
        return exchange(packed((0, heads), 0, kmost))

    def none(over):
        return unwritten((members, 2 * kmost, heads * HDIM))

    sent0 = packed(CHUNKS[0], qslots, KEEP)
    got0 = exchange(sent0)
    sent1, late_weight = after((packed(CHUNKS[1], qslots, KEEP), out_weight))
    weights = own_columns(late_weight, me, groups, half[0])
    got0, *weights = after((got0, *weights))
    over = jnp.max((got0[:, qslots, 0:1] > (DEAD + ALARM) / 2).astype(jnp.int32), axis=0)
    extra = lax.cond(over[0] > 0, whole, none, over)
    sent1, got0, extra, late_weight = after((sent1, got0, extra, late_weight))
    got1 = exchange(sent1)
    weights += own_columns(late_weight, me, groups, half[1])
    gots = got0, got1

    def attended(back):
        which, *chunk = back
        return attend(over, gots[which], extra, CHUNKS[which][0], chunk, qslots, KEEP)

    answer0 = attended(BACK[0])
    answer0, got1, *weights = after((answer0, got1, *weights))
    gots = got0, got1
    back0 = exchange(answer0)
    answer1, back0 = after((attended(BACK[1]), back0))
    back1 = exchange(answer1)
    mine1 = unpack(code, back1)
    mine0 = unpack(code, back0)
    chunk0, chunk1 = BACK[0][1:], BACK[1][1:]

    def items(parts, weights, chunk):
        return [(part, weight, chunk) for part, weight in zip(parts, weights)]

    y0 = along_y(mine0, groups)
    *y0, _ = after((*y0, mine1))
    parts0 = [mine0, *y0, *[swapped(part, groups) for part in (mine0, *y0)]]
    y1 = along_y(mine1, groups)
    total = project(items(parts0, weights, chunk0) + items([mine1], weights, chunk1), None, F32)
    *y1, total = after((*y1, total))
    parts1 = [*y1, *[swapped(part, groups) for part in (mine1, *y1)]]
    return project(items(parts1, weights[1:], chunk1), total, BF16)


def solution(mesh):
    placed = (
        P("ctx", "head"),
        P("ctx", "head"),
        P("ctx", "head"),
        P("ctx", None),
        P("ctx", None),
        P(),
        P("head", None),
    )
    return jax.shard_map(
        per_device, mesh=mesh, in_specs=placed, out_specs=P("ctx", "head"), check_vma=False
    )
```
